32 devices in a mesh: query: 2 (over x), corpus: 16 (over z, y, core).
Axes of the slice: x: 2, y: 2, z: 4, core: 2. Of those that a mesh axis runs over, the one named last changes fastest.
Arguments:
- clean_feats: bfloat16 [2, 2, 512, 320], P('query', None, 'corpus'), may hold values from -6 to 6
- noise_draw: bfloat16 [2, 2, 512, 320], P('query', None, 'corpus'), may hold values from -6 to 6
- timesteps: int32 [2, 2], P('query'), may hold values from 0 to 999
- weight_in: bfloat16 [2, 320, 320], P(None, None, 'corpus'), may hold values from -0.3125 to 0.3125
- weight_ffin: bfloat16 [2, 320, 2560], P(None, None, 'corpus'), may hold values from -0.3125 to 0.3125
- weight_ffout: bfloat16 [2, 1280, 320], P(None, None, 'corpus'), may hold values from -0.15625 to 0.15625
- weight_out: bfloat16 [2, 320, 320], P(None, None, 'corpus'), may hold values from -0.3125 to 0.3125
- norm_gain: float32 [2, 320], replicated, may hold values from 0.5 to 1.5
- norm_bias: float32 [2, 320], replicated, may hold values from -3 to 3
- sketch_cin: bfloat16 [2, 3, 320, 16], replicated, may hold values from -0.3125 to 0.3125
- sketch_fin: bfloat16 [2, 1280, 16], replicated, may hold values from -0.15625 to 0.15625
- sketch_cout: bfloat16 [2, 3, 320, 16], replicated, may hold values from -0.3125 to 0.3125
- sketch_fout: bfloat16 [2, 2560, 16], replicated, may hold values from -0.125 to 0.125
- precond: float32 [8, 256, 256], P('query'), as said below
- store_grads: bfloat16 [8192, 2048], P(('query', 'corpus')), may hold values from -6 to 6
- store_scale: float32 [8192], P(('query', 'corpus')), may hold values from 0.002 to 0.03
Outputs:
- scores: float32 [2, 8192], P(None, ('query', 'corpus'))
The draws below stay inside these ranges and needn't reach their ends.
Inputs may be any that keep to these rules, and one draw needn't show every extreme that they name: `precond`: each layer's matrix is symmetric with a diagonal between 1 and 2.
All inputs are finite; a program needn't handle non-finite values.
Results may differ from the reference program's by a relative error of at most 0.0085.
Values may be sent and summed in bfloat16 or wider, within the bound.
A program may use at most 64 MiB of HBM per device.

```python
import math
import jax
import jax.numpy as jnp
from jax import lax

C = 320
F = 1280
KI = 16
KO = 16
BLOCKS = 2
TSTEPS = 2
K = 256
LAYERS = 8
QUERIES = 2
S = 512
ROWS = 8192


def draw_precond(key, part):
    key_diag, key_off = jax.random.split(jax.random.fold_in(key, 7))
    noise_part = jax.random.normal(key_off, (LAYERS, K, K), jnp.float32)
    symmetric = (noise_part + jnp.swapaxes(noise_part, 1, 2)) * (0.4 / math.sqrt(2.0 * K))
    diagonal = jax.random.uniform(key_diag, (LAYERS, K), jnp.float32, 1.0, 2.0)
    identity_mat = jnp.eye(K, dtype=jnp.float32)
    return symmetric * (1.0 - identity_mat) + identity_mat * diagonal[:, :, None]


def touch_ends(result, stream_key, least, largest):
    longest = result.shape.index(max(result.shape))
    spots = []
    for shift in (0, 1):
        where = [jax.random.randint(jax.random.fold_in(stream_key, axis), (), 0, length) for axis, length in enumerate(result.shape)]
        where[longest] = (where[longest] + shift) % result.shape[longest]
        spots.append(tuple(where))
    return result.at[spots[0]].set(least).at[spots[1]].set(largest)


def levels(own_key, extent, cuts, least, largest):
    factor_of = 1.0
    for dim, blocks in cuts:
        steps = jax.random.uniform(jax.random.fold_in(jax.random.fold_in(own_key, 6), dim), (blocks,), jnp.float32, least / len(cuts), largest / len(cuts))
        factor_of = factor_of * jnp.repeat(jnp.exp(steps), extent[dim] // blocks).reshape((-1,) + (1,) * (len(extent) - 1 - dim))
    return factor_of


def bell_draw(own_key, dims, width, limit, cuts=(), kind=jnp.bfloat16):
    entries = jax.random.normal(own_key, dims, jnp.float32) * width
    if len(cuts) > 0:
        entries = levels(own_key, dims, cuts, -0.22, 0.18) * entries
    return jnp.clip(entries, min=-limit, max=limit).astype(kind)


def setup_inputs(seed: int = 0) -> dict:
    arg_keys = jax.random.split(jax.random.key(seed), 17)
    return {
        "clean_feats": bell_draw(arg_keys[0], (QUERIES, TSTEPS, S, C), 1.0, 6.0, ((0, 2), (2, 16))),
        "noise_draw": bell_draw(arg_keys[1], (QUERIES, TSTEPS, S, C), 1.0, 6.0, ((0, 2), (2, 16))),
        "timesteps": touch_ends(jax.random.randint(arg_keys[2], (QUERIES, TSTEPS), 0, 1000), jax.random.fold_in(arg_keys[2], 1), 0, 999).astype(jnp.int32),
        "weight_in": bell_draw(arg_keys[3], (BLOCKS, C, C), C ** -0.5, 0.3125, ((2, 16),)),
        "weight_ffin": bell_draw(arg_keys[4], (BLOCKS, C, 2 * F), C ** -0.5, 0.3125, ((2, 16),)),
        "weight_ffout": bell_draw(arg_keys[5], (BLOCKS, F, C), F ** -0.5, 0.15625, ((2, 16),)),
        "weight_out": bell_draw(arg_keys[6], (BLOCKS, C, C), C ** -0.5, 0.3125, ((2, 16),)),
        "norm_gain": jnp.clip(1.0 + 0.1 * jax.random.normal(arg_keys[7], (BLOCKS, C), jnp.float32), 0.5, 1.5),
        "norm_bias": bell_draw(arg_keys[8], (BLOCKS, C), 0.5, 3.0, (), jnp.float32),
        "sketch_cin": bell_draw(arg_keys[9], (BLOCKS, 3, C, KI), C ** -0.5, 0.3125),
        "sketch_fin": bell_draw(arg_keys[10], (BLOCKS, F, KI), F ** -0.5, 0.15625),
        "sketch_cout": bell_draw(arg_keys[11], (BLOCKS, 3, C, KO), C ** -0.5, 0.3125),
        "sketch_fout": bell_draw(arg_keys[12], (BLOCKS, 2 * F, KO), (2 * F) ** -0.5, 0.125),
        "precond": draw_precond(jax.random.fold_in(arg_keys[16], 71), 0),
        "store_grads": bell_draw(arg_keys[14], (ROWS, LAYERS * K), 1.0, 6.0, ((0, 32),)),
        "store_scale": jnp.clip(jnp.exp(math.log(0.03) - 2.70805 * jax.random.uniform(arg_keys[15], (ROWS,), jnp.float32) ** levels(arg_keys[15], (ROWS,), ((0, 32),), -0.2, 0.2)), 0.002, 0.03),
    }


plan_len = 1000

def noise_levels(timesteps):
    steps = jnp.arange(plan_len, dtype=jnp.float32)
    rooted = math.sqrt(0.00085) + (math.sqrt(0.012) - math.sqrt(0.00085)) * steps / (plan_len - 1)
    cumulative = jnp.exp(jnp.cumsum(jnp.log1p(-rooted * rooted)))
    matches = timesteps[..., None] == jnp.arange(plan_len, dtype=jnp.int32)
    picked = lax.optimization_barrier(jnp.sum(jnp.where(matches, cumulative, jnp.zeros_like(cumulative)), axis=-1))
    return (jnp.sqrt(picked), jnp.sqrt(1.0 - picked))

def gelu_parts(gate):
    cumul = 0.5 * (1.0 + jax.scipy.special.erf(gate / math.sqrt(2.0)))
    density = jnp.exp(-0.5 * gate * gate) / math.sqrt(2.0 * math.pi)
    return (gate * cumul, cumul + gate * density)

def contract_back(delta, weight):
    return lax.dot_general(delta, weight, (((1,), (1,)), ((), ())), preferred_element_type=jnp.float32)

def block_forward(residual_stream, weights, scale_gain, shift_bias):
    weight_in, weight_ffin, weight_ffout, weight_out = weights
    hidden = weight_ffout.shape[0]
    residual_reduced = residual_stream.astype(jnp.bfloat16)
    inner = jnp.dot(residual_reduced, weight_in, preferred_element_type=jnp.float32)
    centred_input = inner - lax.optimization_barrier(jnp.mean(inner, axis=-1, keepdims=True))
    inverse_deviation = lax.rsqrt(lax.optimization_barrier(jnp.mean(centred_input * centred_input, axis=-1, keepdims=True)) + 1e-05)
    standardized_input = centred_input * inverse_deviation
    normalized_input = (standardized_input * scale_gain + shift_bias).astype(jnp.bfloat16)
    projected = jnp.dot(normalized_input, weight_ffin, preferred_element_type=jnp.float32)
    value_output = projected[:, :hidden]
    gate = projected[:, hidden:]
    gelu_result, gelu_derivative = gelu_parts(gate)
    mixed_hidden = (value_output * gelu_result).astype(jnp.bfloat16)
    inner_two = inner + jnp.dot(mixed_hidden, weight_ffout, preferred_element_type=jnp.float32)
    inner_reduced = inner_two.astype(jnp.bfloat16)
    residual_stream = residual_stream + jnp.dot(inner_reduced, weight_out, preferred_element_type=jnp.float32)
    return (residual_stream, (residual_reduced, standardized_input, inverse_deviation, normalized_input, value_output, gelu_result, gelu_derivative, mixed_hidden, inner_reduced))

def block_backward(dstream, saved_activations, weights, scale_gain):
    weight_in, weight_ffin, weight_ffout, weight_out = weights
    residual_reduced, standardized_input, inverse_deviation, normalized_input, value_output, gelu_result, gelu_derivative, mixed_hidden, inner_reduced = saved_activations
    dout_low = dstream.astype(jnp.bfloat16)
    second_inner_gradient = contract_back(dout_low, weight_out)
    dtwo_low = second_inner_gradient.astype(jnp.bfloat16)
    dmixed = contract_back(dtwo_low, weight_ffout)
    dproj_low = jnp.concatenate([dmixed * gelu_result, dmixed * value_output * gelu_derivative], axis=-1).astype(jnp.bfloat16)
    dnormed = contract_back(dproj_low, weight_ffin)
    scaled_hidden = dnormed * scale_gain
    inner_gradient = second_inner_gradient + inverse_deviation * (scaled_hidden - lax.optimization_barrier(jnp.mean(scaled_hidden, axis=-1, keepdims=True)) - standardized_input * lax.optimization_barrier(jnp.mean(scaled_hidden * standardized_input, axis=-1, keepdims=True)))
    dinner_low = inner_gradient.astype(jnp.bfloat16)
    dstream = dstream + contract_back(dinner_low, weight_in)
    records = [(residual_reduced, dinner_low), (normalized_input, dproj_low), (mixed_hidden, dtwo_low), (inner_reduced, dout_low)]
    return (dstream, records)

def project_layer(inputs, deltas, sketch_in, sketch_out, samples):
    left = jnp.dot(inputs, sketch_in, preferred_element_type=jnp.float32)
    right = jnp.dot(deltas, sketch_out, preferred_element_type=jnp.float32)
    left = left.reshape(samples, -1, left.shape[-1])
    right = right.reshape(samples, -1, right.shape[-1])
    outer = jnp.einsum('srk,srj->skj', left, right, precision=lax.Precision.HIGHEST)
    return outer.reshape(samples, -1)

def sketches_of(block, sketch_cin, sketch_fin, sketch_cout, sketch_fout):
    return [(sketch_cin[block, 0], sketch_cout[block, 0]), (sketch_cin[block, 1], sketch_fout[block]), (sketch_fin[block], sketch_cout[block, 1]), (sketch_cin[block, 2], sketch_cout[block, 2])]

def reference(clean_feats, noise_draw, timesteps, weight_in, weight_ffin, weight_ffout, weight_out, norm_gain, norm_bias, sketch_cin, sketch_fin, sketch_cout, sketch_fout, precond, store_grads, store_scale):
    signal, spread = noise_levels(timesteps)
    loss_scale = 1.0 / math.sqrt(TSTEPS * S)
    blocks = weight_in.shape[0]

    def one_query(packed):
        clean_one, noise_one, signal_one, spread_one = packed
        noise_rows = noise_one.astype(jnp.float32)
        residual_stream = signal_one[:, None, None] * clean_one.astype(jnp.float32) + spread_one[:, None, None] * noise_rows
        residual_stream = residual_stream.reshape(-1, residual_stream.shape[-1])
        noise_rows = noise_rows.reshape(-1, noise_rows.shape[-1])
        saved_all = []
        for block in range(blocks):
            weights = (weight_in[block], weight_ffin[block], weight_ffout[block], weight_out[block])
            residual_stream, saved_activations = block_forward(residual_stream, weights, norm_gain[block], norm_bias[block])
            saved_all.append(saved_activations)
        dstream = (residual_stream - noise_rows) * loss_scale
        layers = [None] * (4 * blocks)
        for block in reversed(range(blocks)):
            weights = (weight_in[block], weight_ffin[block], weight_ffout[block], weight_out[block])
            dstream, records = block_backward(dstream, saved_all[block], weights, norm_gain[block])
            pairs = sketches_of(block, sketch_cin, sketch_fin, sketch_cout, sketch_fout)
            for index in range(4):
                layers[4 * block + index] = project_layer(records[index][0], records[index][1], pairs[index][0], pairs[index][1], 1)[0]
        return jnp.stack(layers, axis=0)
    grads = lax.map(one_query, (clean_feats, noise_draw, signal, spread))
    pre = jnp.einsum('qlk,lkj->qlj', grads, precond, precision=lax.Precision.HIGHEST).astype(jnp.bfloat16)
    flat = pre.reshape(pre.shape[0], -1)
    raw = lax.dot_general(flat, store_grads, (((1,), (1,)), ((), ())), preferred_element_type=jnp.float32)
    return raw * store_scale[None, :]
```

```python
import math

import jax
import jax.numpy as jnp
from jax import lax
from jax.sharding import PartitionSpec as P

plan_len = 1000


def noise_levels(timesteps):
    steps = jnp.arange(plan_len, dtype=jnp.float32)
    rooted = math.sqrt(0.00085) + (math.sqrt(0.012) - math.sqrt(0.00085)) * steps / (plan_len - 1)
    terms = jnp.log1p(-rooted * rooted)
    reached = jnp.arange(plan_len, dtype=jnp.int32) <= timesteps[..., None]
    picked = jnp.exp(jnp.sum(jnp.where(reached, terms, jnp.zeros_like(terms)), axis=-1))
    return (jnp.sqrt(picked), jnp.sqrt(1.0 - picked))


def gelu_parts(gate):
    cumul = 0.5 * (1.0 + jax.scipy.special.erf(gate / math.sqrt(2.0)))
    density = jnp.exp(-0.5 * gate * gate) / math.sqrt(2.0 * math.pi)
    return (gate * cumul, cumul + gate * density)


def contract_back(delta, weight):
    return lax.dot_general(
        delta, weight, (((1,), (1,)), ((), ())), preferred_element_type=jnp.float32
    )


def block_forward(residual_stream, weights, scale_gain, shift_bias):
    weight_in, weight_ffin, weight_ffout, weight_out = weights
    hidden = weight_ffout.shape[0]
    residual_reduced = residual_stream.astype(jnp.bfloat16)
    inner = jnp.dot(residual_reduced, weight_in, preferred_element_type=jnp.float32)
    centred_input = inner - jnp.mean(inner, axis=-1, keepdims=True)
    inverse_deviation = lax.rsqrt(
        jnp.mean(centred_input * centred_input, axis=-1, keepdims=True) + 1e-05
    )
    standardized_input = centred_input * inverse_deviation
    normalized_input = (standardized_input * scale_gain + shift_bias).astype(jnp.bfloat16)
    projected = jnp.dot(normalized_input, weight_ffin, preferred_element_type=jnp.float32)
    value_output = projected[:, :hidden]
    gate = projected[:, hidden:]
    gelu_result, gelu_derivative = gelu_parts(gate)
    mixed_hidden = (value_output * gelu_result).astype(jnp.bfloat16)
    inner_two = inner + jnp.dot(mixed_hidden, weight_ffout, preferred_element_type=jnp.float32)
    inner_reduced = inner_two.astype(jnp.bfloat16)
    residual_stream = residual_stream + jnp.dot(
        inner_reduced, weight_out, preferred_element_type=jnp.float32
    )
    return (
        residual_stream,
        (
            residual_reduced,
            standardized_input,
            inverse_deviation,
            normalized_input,
            value_output,
            gelu_result,
            gelu_derivative,
            mixed_hidden,
            inner_reduced,
        ),
    )


def block_backward(dstream, saved_activations, weights, scale_gain):
    weight_in, weight_ffin, weight_ffout, weight_out = weights
    (
        residual_reduced,
        standardized_input,
        inverse_deviation,
        normalized_input,
        value_output,
        gelu_result,
        gelu_derivative,
        mixed_hidden,
        inner_reduced,
    ) = saved_activations
    dout_low = dstream.astype(jnp.bfloat16)
    second_inner_gradient = contract_back(dout_low, weight_out)
    dtwo_low = second_inner_gradient.astype(jnp.bfloat16)
    dmixed = contract_back(dtwo_low, weight_ffout)
    dproj_low = jnp.concatenate(
        [dmixed * gelu_result, dmixed * value_output * gelu_derivative], axis=-1
    ).astype(jnp.bfloat16)
    dnormed = contract_back(dproj_low, weight_ffin)
    scaled_hidden = dnormed * scale_gain
    inner_gradient = second_inner_gradient + inverse_deviation * (
        scaled_hidden
        - jnp.mean(scaled_hidden, axis=-1, keepdims=True)
        - standardized_input * jnp.mean(scaled_hidden * standardized_input, axis=-1, keepdims=True)
    )
    dinner_low = inner_gradient.astype(jnp.bfloat16)
    dstream = dstream + contract_back(dinner_low, weight_in)
    records = [
        (residual_reduced, dinner_low),
        (normalized_input, dproj_low),
        (mixed_hidden, dtwo_low),
        (inner_reduced, dout_low),
    ]
    return (dstream, records)


def project_layer(inputs, deltas, sketch_in, sketch_out, samples):
    left = jnp.dot(inputs, sketch_in, preferred_element_type=jnp.float32)
    right = jnp.dot(deltas, sketch_out, preferred_element_type=jnp.float32)
    left = left.reshape(samples, -1, left.shape[-1])
    right = right.reshape(samples, -1, right.shape[-1])
    outer = jnp.einsum("srk,srj->skj", left, right, precision=lax.Precision.HIGHEST)
    return outer.reshape(samples, -1)


def sketches_of(block, sketch_cin, sketch_fin, sketch_cout, sketch_fout):
    return [
        (sketch_cin[block, 0], sketch_cout[block, 0]),
        (sketch_cin[block, 1], sketch_fout[block]),
        (sketch_fin[block], sketch_cout[block, 1]),
        (sketch_cin[block, 2], sketch_cout[block, 2]),
    ]


def on_device(
    clean_feats,
    noise_draw,
    timesteps,
    weight_in,
    weight_ffin,
    weight_ffout,
    weight_out,
    norm_gain,
    norm_bias,
    sketch_cin,
    sketch_fin,
    sketch_cout,
    sketch_fout,
    precond,
    store_grads,
    store_scale,
):
    samples = clean_feats.shape[0]
    positions = clean_feats.shape[2] * lax.axis_size("corpus")
    loss_scale = 1.0 / math.sqrt(clean_feats.shape[1] * positions)
    blocks = weight_in.shape[0]
    signal, spread = noise_levels(timesteps)
    noise_rows = noise_draw.astype(jnp.float32)
    residual_stream = (
        signal[:, :, None, None] * clean_feats.astype(jnp.float32)
        + spread[:, :, None, None] * noise_rows
    )
    residual_stream = residual_stream.reshape(-1, residual_stream.shape[-1])
    noise_rows = noise_rows.reshape(-1, noise_rows.shape[-1])
    gathered = (
        lax.all_gather(weight_in, "corpus", axis=2, tiled=True),
        lax.all_gather(weight_ffin, "corpus", axis=2, tiled=True),
        lax.all_gather(weight_ffout, "corpus", axis=2, tiled=True),
        lax.all_gather(weight_out, "corpus", axis=2, tiled=True),
    )

    def fetch_forward(block):
        return tuple((member[block] for member in gathered))

    def fetch_backward(block):
        return tuple((member[block] for member in gathered))

    saved_all = []
    for block in range(blocks):
        residual_stream, saved_activations = block_forward(
            residual_stream, fetch_forward(block), norm_gain[block], norm_bias[block]
        )
        saved_all.append(saved_activations)
    dstream = (residual_stream - noise_rows) * loss_scale
    layers = [None] * (4 * blocks)
    for block in reversed(range(blocks)):
        dstream, records = block_backward(
            dstream, saved_all[block], fetch_backward(block), norm_gain[block]
        )
        pairs = sketches_of(block, sketch_cin, sketch_fin, sketch_cout, sketch_fout)
        for index in range(4):
            layers[4 * block + index] = project_layer(
                records[index][0], records[index][1], pairs[index][0], pairs[index][1], samples
            )
    partial_grads = jnp.stack(layers, axis=1)
    totals = lax.psum(partial_grads, "corpus")
    routed = lax.all_to_all(totals, "query", split_axis=1, concat_axis=0, tiled=True)
    owned = jnp.einsum("qlk,lkj->qlj", routed, precond, precision=lax.Precision.HIGHEST).astype(
        jnp.bfloat16
    )
    preconditioned = lax.all_gather(owned, "query", axis=1, tiled=True)
    flat = preconditioned.reshape(preconditioned.shape[0], -1)
    raw = lax.dot_general(
        flat, store_grads, (((1,), (1,)), ((), ())), preferred_element_type=jnp.float32
    )
    return raw * store_scale[None, :]


def solution(mesh):
    placed = (
        P("query", None, "corpus", None),
        P("query", None, "corpus", None),
        P("query", None),
        P(None, None, "corpus"),
        P(None, None, "corpus"),
        P(None, None, "corpus"),
        P(None, None, "corpus"),
        P(),
        P(),
        P(),
        P(),
        P(),
        P(),
        P("query", None, None),
        P(("query", "corpus"), None),
        P(("query", "corpus")),
    )
    return jax.shard_map(
        on_device,
        mesh=mesh,
        in_specs=placed,
        out_specs=P(None, ("query", "corpus")),
        check_vma=False,
    )
```

```python
import math

import jax
import jax.numpy as jnp
from jax import lax
from jax.experimental import pallas as pl
from jax.experimental.pallas import tpu as pltpu
from jax.sharding import PartitionSpec as P

plan_len = 1000


def noise_levels(timesteps):
    steps = jnp.arange(plan_len, dtype=jnp.float32)
    rooted = math.sqrt(0.00085) + (math.sqrt(0.012) - math.sqrt(0.00085)) * steps / (plan_len - 1)
    terms = jnp.log1p(-rooted * rooted)
    reached = jnp.arange(plan_len, dtype=jnp.int32) <= timesteps[..., None]
    picked = jnp.exp(jnp.sum(jnp.where(reached, terms, jnp.zeros_like(terms)), axis=-1))
    return (jnp.sqrt(picked), jnp.sqrt(1.0 - picked))


def gelu_parts(gate):
    cumul = 0.5 * (1.0 + jax.scipy.special.erf(gate / math.sqrt(2.0)))
    density = jnp.exp(-0.5 * gate * gate) / math.sqrt(2.0 * math.pi)
    return (gate * cumul, cumul + gate * density)


def contract_back(delta, weight):
    return lax.dot_general(
        delta, weight, (((1,), (1,)), ((), ())), preferred_element_type=jnp.float32
    )


def block_forward(residual_stream, weights, scale_gain, shift_bias):
    weight_in, weight_ffin, weight_ffout, weight_out = weights
    hidden = weight_ffout.shape[0]
    residual_reduced = residual_stream.astype(jnp.bfloat16)
    inner = jnp.dot(residual_reduced, weight_in, preferred_element_type=jnp.float32)
    centred_input = inner - jnp.mean(inner, axis=-1, keepdims=True)
    inverse_deviation = lax.rsqrt(
        jnp.mean(centred_input * centred_input, axis=-1, keepdims=True) + 1e-05
    )
    standardized_input = centred_input * inverse_deviation
    normalized_input = (standardized_input * scale_gain + shift_bias).astype(jnp.bfloat16)
    projected = jnp.dot(normalized_input, weight_ffin, preferred_element_type=jnp.float32)
    value_output = projected[:, :hidden]
    gate = projected[:, hidden:]
    gelu_result, gelu_derivative = gelu_parts(gate)
    mixed_hidden = (value_output * gelu_result).astype(jnp.bfloat16)
    inner_two = inner + jnp.dot(mixed_hidden, weight_ffout, preferred_element_type=jnp.float32)
    inner_reduced = inner_two.astype(jnp.bfloat16)
    residual_stream = residual_stream + jnp.dot(
        inner_reduced, weight_out, preferred_element_type=jnp.float32
    )
    return (
        residual_stream,
        (
            residual_reduced,
            standardized_input,
            inverse_deviation,
            normalized_input,
            value_output,
            gelu_result,
            gelu_derivative,
            mixed_hidden,
            inner_reduced,
        ),
    )


def block_backward(dstream, saved_activations, weights, scale_gain):
    weight_in, weight_ffin, weight_ffout, weight_out = weights
    (
        residual_reduced,
        standardized_input,
        inverse_deviation,
        normalized_input,
        value_output,
        gelu_result,
        gelu_derivative,
        mixed_hidden,
        inner_reduced,
    ) = saved_activations
    dout_low = dstream.astype(jnp.bfloat16)
    second_inner_gradient = contract_back(dout_low, weight_out)
    dtwo_low = second_inner_gradient.astype(jnp.bfloat16)
    dmixed = contract_back(dtwo_low, weight_ffout)
    dproj_low = jnp.concatenate(
        [dmixed * gelu_result, dmixed * value_output * gelu_derivative], axis=-1
    ).astype(jnp.bfloat16)
    dnormed = contract_back(dproj_low, weight_ffin)
    scaled_hidden = dnormed * scale_gain
    inner_gradient = second_inner_gradient + inverse_deviation * (
        scaled_hidden
        - jnp.mean(scaled_hidden, axis=-1, keepdims=True)
        - standardized_input * jnp.mean(scaled_hidden * standardized_input, axis=-1, keepdims=True)
    )
    dinner_low = inner_gradient.astype(jnp.bfloat16)
    dstream = dstream + contract_back(dinner_low, weight_in)
    records = [
        (residual_reduced, dinner_low),
        (normalized_input, dproj_low),
        (mixed_hidden, dtwo_low),
        (inner_reduced, dout_low),
    ]
    return (dstream, records)


def project_layer(inputs, deltas, sketch_in, sketch_out, samples):
    left = jnp.dot(inputs, sketch_in, preferred_element_type=jnp.float32)
    right = jnp.dot(deltas, sketch_out, preferred_element_type=jnp.float32)
    left = left.reshape(samples, -1, left.shape[-1])
    right = right.reshape(samples, -1, right.shape[-1])
    outer = jnp.einsum("srk,srj->skj", left, right, precision=lax.Precision.HIGHEST)
    return outer.reshape(samples, -1)


def sketches_of(block, sketch_cin, sketch_fin, sketch_cout, sketch_fout):
    return [
        (sketch_cin[block, 0], sketch_cout[block, 0]),
        (sketch_cin[block, 1], sketch_fout[block]),
        (sketch_fin[block], sketch_cout[block, 1]),
        (sketch_cin[block, 2], sketch_cout[block, 2]),
    ]


def on_device(
    clean_feats,
    noise_draw,
    timesteps,
    weight_in,
    weight_ffin,
    weight_ffout,
    weight_out,
    norm_gain,
    norm_bias,
    sketch_cin,
    sketch_fin,
    sketch_cout,
    sketch_fout,
    precond,
    store_grads,
    store_scale,
):
    samples = clean_feats.shape[0]
    positions = clean_feats.shape[2] * lax.axis_size("corpus")
    loss_scale = 1.0 / math.sqrt(clean_feats.shape[1] * positions)
    blocks = weight_in.shape[0]
    signal, spread = noise_levels(timesteps)
    noise_rows = noise_draw.astype(jnp.float32)
    residual_stream = (
        signal[:, :, None, None] * clean_feats.astype(jnp.float32)
        + spread[:, :, None, None] * noise_rows
    )
    residual_stream = residual_stream.reshape(-1, residual_stream.shape[-1])
    noise_rows = noise_rows.reshape(-1, noise_rows.shape[-1])
    gathered = (
        lax.all_gather(weight_in, "corpus", axis=2, tiled=True),
        lax.all_gather(weight_ffin, "corpus", axis=2, tiled=True),
        lax.all_gather(weight_ffout, "corpus", axis=2, tiled=True),
        lax.all_gather(weight_out, "corpus", axis=2, tiled=True),
    )

    def fetch_forward(block):
        return tuple((member[block] for member in gathered))

    def fetch_backward(block):
        return tuple((member[block] for member in gathered))

    saved_all = []
    for block in range(blocks):
        residual_stream, saved_activations = block_forward(
            residual_stream, fetch_forward(block), norm_gain[block], norm_bias[block]
        )
        saved_all.append(saved_activations)
    dstream = (residual_stream - noise_rows) * loss_scale
    layers = [None] * (4 * blocks)
    for block in reversed(range(blocks)):
        dstream, records = block_backward(
            dstream, saved_all[block], fetch_backward(block), norm_gain[block]
        )
        pairs = sketches_of(block, sketch_cin, sketch_fin, sketch_cout, sketch_fout)
        for index in range(4):
            layers[4 * block + index] = project_layer(
                records[index][0], records[index][1], pairs[index][0], pairs[index][1], samples
            )
    partial_grads = jnp.stack(layers, axis=1)
    totals = lax.psum(partial_grads, "corpus")
    routed = lax.all_to_all(totals, "query", split_axis=1, concat_axis=0, tiled=True)
    owned = jnp.einsum("qlk,lkj->qlj", routed, precond, precision=lax.Precision.HIGHEST).astype(
        jnp.bfloat16
    )
    preconditioned = lax.all_gather(owned, "query", axis=1, tiled=True)
    flat = preconditioned.reshape(preconditioned.shape[0], -1)
    raw = lax.dot_general(
        flat, store_grads, (((1,), (1,)), ((), ())), preferred_element_type=jnp.float32
    )
    return raw * store_scale[None, :]


MESH = pl.DeviceIdType.MESH
f32 = jnp.float32
bf16 = jnp.bfloat16
zs_n, ys_n, cores, ranks = 4, 2, 2, 16
small = 128
wide = 160
slot = small + wide
half = slot // 2
lanes = 384
strips = 4


def dot(a, b, dims=((1,), (0,)), precision=None):
    return lax.dot_general(a, b, (dims, ((), ())), preferred_element_type=f32, precision=precision)


def dot_t(a, b):
    return dot(a, b, ((1,), (1,)))


def one_hot(shape, fn):
    r = lax.broadcasted_iota(jnp.int32, shape, 0)
    c = lax.broadcasted_iota(jnp.int32, shape, 1)
    return fn(r, c).astype(f32).astype(bf16)


def kernel(
    steps_ref, clean_ref, noise_ref, win_ref, wfi_ref, wfo_ref, wout_ref, gain_ref, bias_ref,
    cin_ref, fin_ref, cout_ref, fout_ref, precond_hbm, store_hbm, raw_ref,
    w, d, dfo, clean_p, noise_p, gain_p, bias_p, ecin, efin, ecout, efout, xin_s, xhat_s, isig_s, norm_s, gel_s, der_s, mix_s, xout_s,
    part, box, pre, precond, store,
    send, recv, all_send, all_recv, pre_send, pre_recv, local,
):
    x = lax.axis_index("query")
    me = lax.axis_index("corpus")
    z = me // (ys_n * cores)
    y = (me // cores) % ys_n
    k = me % cores
    flat = x * ranks + me
    devices = 2 * ranks
    share = win_ref.shape[2]

    barrier = pltpu.get_barrier_semaphore()

    @pl.loop(0, devices)
    def _(i):
        @pl.when(i != flat)
        def _():
            pl.semaphore_signal(barrier, inc=1, device_id=(i // ranks, i % ranks), device_id_type=MESH)

    fetch_p = pltpu.make_async_copy(precond_hbm, precond, local.at[0])
    fetch_s = pltpu.make_async_copy(store_hbm, store, local.at[1])
    fetch_p.start()
    fetch_s.start()

    places = [
        one_hot((small, share), lambda r, c, s=s: r == share * s + c) for s in range(2 + strips)
    ]
    same = one_hot((wide, wide), lambda r, c: r == c)
    channels, hidden = win_ref.shape[1], fin_ref.shape[1]

    def tall(v):
        if v.shape[0] == lanes:
            return v
        return jnp.concatenate([v, jnp.zeros((lanes - v.shape[0], v.shape[1]), v.dtype)], axis=0)

    for b in range(2):
        rows = dot_t(places[0], tall(win_ref[b])) + dot_t(places[1], tall(wout_ref[b]))
        for s in range(strips):
            rows += dot_t(places[2 + s], tall(wfo_ref[b, lanes * s : min(lanes * (s + 1), hidden), :]))
        w[b, me, 0:small, :] = rows.astype(bf16)
        w[b, me, small:slot, :] = dot_t(same, tall(wfi_ref[b])).astype(bf16)

    pl.semaphore_wait(barrier, devices - 1)

    def src_of(zs, yy):
        return (zs * ys_n + yy) * cores + k

    def unit(b, src, p):
        return w.at[b, src, pl.ds(pl.multiple_of(p * half, 16), half)]

    def copy(kind, b, src, p, qd, cd):
        return pltpu.make_async_remote_copy(
            src_ref=unit(b, src, p), dst_ref=unit(b, src, p),
            send_sem=send.at[kind, b, src, p], recv_sem=recv.at[b, src, p],
            device_id=(qd, cd), device_id_type=MESH,
        )

    started = []

    def start(guard, *what):
        started.append((guard, what))
        if guard is None:
            copy(*what).start()
        else:
            @pl.when(guard)
            def _():
                copy(*what).start()

    def arrive(guard, b, src, p):
        def go():
            copy(0, b, src, p, x, me ^ 1).wait_recv()
        if guard is None:
            go()
        else:
            pl.when(guard)(go)

    up, down = me + ys_n * cores, me - ys_n * cores
    beside, twin = me + cores * (1 - 2 * y), me + 1 - 2 * k
    far = 1 - x

    def both(guard, more):
        return more if guard is None else jnp.logical_and(guard, more)

    def direct(b, dist):
        sides = [(0, 0)] if dist == 0 else [(-1, 1), (1, 1)]
        for side, _ in sides:
            zs = z + side * dist
            ok = None if dist == 0 else jnp.logical_and(zs >= 0, zs < zs_n)
            src = src_of(zs, y)
            for p in range(2):
                if dist:
                    arrive(ok, b, src, p)
                if side <= 0:
                    start(both(ok, z < zs_n - 1), 0, b, src, p, x, up)
                if side >= 0:
                    start(both(ok, z > 0), 1, b, src, p, x, down)
                start(ok, 3, b, src, p, x, twin)
            start(ok, 2, b, src, x, x, beside)

    def cross(b, dist, relayed):
        for side in ([0] if dist == 0 else [-1, 1]):
            zs = z + side * dist
            ok = None if dist == 0 else jnp.logical_and(zs >= 0, zs < zs_n)
            src = src_of(zs, 1 - y)
            if relayed:
                arrive(ok, b, src, 1 - x)
                start(ok, 3, b, src, 1 - x, x, twin)
            else:
                arrive(ok, b, src, x)
                start(ok, 2, b, src, x, far, me)
                start(ok, 3, b, src, x, x, twin)

    def block_steps(b):
        return [
            lambda: direct(b, 0),
            lambda: direct(b, 1),
            lambda: (cross(b, 0, False), direct(b, 2)),
            lambda: (cross(b, 1, False), direct(b, 3), cross(b, 0, True)),
            lambda: (cross(b, 2, False), cross(b, 1, True)),
            lambda: (cross(b, 3, False), cross(b, 2, True)),
            lambda: cross(b, 3, True),
        ]

    def twins(b):
        for i in range(zs_n * ys_n):
            for p in range(2):
                arrive(None, b, i * cores + (1 - k), p)

    ki = cin_ref.shape[-1]
    spread_in = one_hot((ki * ki, ki), lambda r, c: c == r // ki)
    spread_out = one_hot((ki * ki, ki), lambda r, c: c == r % ki)

    def spread_c(b):
        for j in range(3):
            ecin[b, j] = dot_t(spread_in, tall(cin_ref[b, j])).astype(bf16)
            ecout[b, j] = dot_t(spread_out, tall(cout_ref[b, j])).astype(bf16)

    def spread_f(b):
        efin[b] = dot_t(spread_in, fin_ref[b]).astype(bf16)
        for s in range(2):
            cut = slice(hidden * s, hidden * (s + 1))
            efout[b, s] = dot_t(spread_out, fout_ref[b, cut]).astype(bf16)

    def widen():
        for wide_ref, narrow in ((clean_p, clean_ref), (noise_p, noise_ref), (gain_p, gain_ref), (bias_p, bias_ref)):
            wide_ref[...] = jnp.zeros_like(wide_ref)
            wide_ref[:, 0:channels] = narrow[...]
        for b in range(2):
            for j in range(2):
                d[b, j, channels:lanes, :] = jnp.zeros((lanes - channels, lanes), bf16)
            dfo[b, channels:lanes, :] = jnp.zeros((lanes - channels, hidden), bf16)

    group = 4
    outs = group * share
    many = 2 + strips

    def unpack(b):
        pick = jnp.concatenate(
            [
                one_hot(
                    (outs, group * small),
                    lambda r, c, s=s: c == (r // share) * small + share * s + r % share,
                )
                for s in range(many)
            ],
            axis=0,
        )
        for g in range(ranks // group):
            got = dot(pick, w[b, group * g : group * (g + 1), 0:small, :].reshape(group * small, lanes)).astype(bf16)
            for s in range(2):
                d[b, s, outs * g : outs * (g + 1), :] = got[outs * s : outs * (s + 1)]
            for s in range(strips):
                end = min(lanes * (s + 1), hidden)
                dfo[b, outs * g : outs * (g + 1), lanes * s : end] = got[
                    outs * (2 + s) : outs * (3 + s), 0 : end - lanes * s
                ]

    def ffin(b, s):
        return w[b, ranks // 2 * s : ranks // 2 * (s + 1), small:slot, :].reshape(hidden, lanes)

    rows_each = clean_ref.shape[0] // 2
    rows = 2 * rows_each
    live = lax.broadcasted_iota(jnp.int32, (1, lanes), 1) < channels

    def mean(v):
        return jnp.sum(v, axis=-1, keepdims=True) * (1.0 / channels)

    def levels():
        order = (
            lax.broadcasted_iota(jnp.int32, (8, 128), 0) * 128 + lax.broadcasted_iota(jnp.int32, (8, 128), 1)
        )
        rooted = math.sqrt(0.00085) + (math.sqrt(0.012) - math.sqrt(0.00085)) * order.astype(f32) / (plan_len - 1)
        terms = jnp.log1p(-rooted * rooted)
        first = lax.broadcasted_iota(jnp.int32, (rows, 1), 0) < rows_each
        total = [
            jnp.sum(jnp.where(order <= steps_ref[t], terms, 0.0), axis=(0, 1), keepdims=True) for t in range(2)
        ]
        kept = jnp.exp(jnp.where(first, total[0], total[1]))
        return jnp.sqrt(kept), jnp.sqrt(1.0 - kept)

    def forward(b, stream):
        xin = stream.astype(bf16)
        xin_s[b] = xin
        inner = dot_t(xin, d[b, 0])
        centred = jnp.where(live, inner - mean(inner), 0.0)
        inv = lax.rsqrt(mean(centred * centred) + 1e-05)
        xhat = centred * inv
        xhat_s[b] = xhat
        isig_s[b] = inv
        normed = (xhat * gain_p[b : b + 1] + bias_p[b : b + 1]).astype(bf16)
        norm_s[b] = normed
        value = dot_t(normed, ffin(b, 0))
        gate = dot_t(normed, ffin(b, 1))
        cumul = 0.5 * (1.0 + lax.erf(gate * (1.0 / math.sqrt(2.0))))
        density = jnp.exp(-0.5 * gate * gate) * (1.0 / math.sqrt(2.0 * math.pi))
        gel = gate * cumul
        gel_s[b] = gel
        der_s[b] = value * (cumul + gate * density)
        mixed = (value * gel).astype(bf16)
        mix_s[b] = mixed
        inner += dot_t(mixed, dfo[b])
        xout = inner.astype(bf16)
        xout_s[b] = xout
        return stream + dot_t(xout, d[b, 1])

    def record(layer, left, right):
        part[layer // 4, layer % 4 : layer % 4 + 1, :] = jnp.sum(left * right, axis=0, keepdims=True)

    def backward(b, ds):
        dout = ds.astype(bf16)
        d2 = dot(dout, d[b, 1])
        d2b = d2.astype(bf16)
        dmix = dot(d2b, dfo[b])
        dval = (dmix * gel_s[b]).astype(bf16)
        dgate = (dmix * der_s[b]).astype(bf16)
        dnorm = dot(dval, ffin(b, 0)) + dot(dgate, ffin(b, 1))
        right = dot_t(dval, efout[b, 0]) + dot_t(dgate, efout[b, 1])
        left = dot_t(mix_s[b], efin[b])
        g = dnorm * gain_p[b : b + 1]
        xhat = xhat_s[b]
        dinner = jnp.where(live, d2 + isig_s[b] * (g - mean(g) - xhat * mean(g * xhat)), 0.0)
        dinb = dinner.astype(bf16)
        record(4 * b + 1, dot_t(norm_s[b], ecin[b, 1]), right)
        record(4 * b + 2, left, dot_t(d2b, ecout[b, 1]))
        record(4 * b + 3, dot_t(xout_s[b], ecin[b, 2]), dot_t(dout, ecout[b, 2]))
        record(4 * b, dot_t(xin_s[b], ecin[b, 0]), dot_t(dinb, ecout[b, 0]))
        return ds + dot(dinb, d[b, 0]) if b else None

    first, second = block_steps(0), block_steps(1)
    lag = 2
    fill = [widen, lambda: spread_c(0), lambda: spread_c(1), lambda: spread_f(0), lambda: spread_f(1)]
    for i in range(len(first) + lag):
        if i < len(first):
            first[i]()
        if 0 <= i - lag < len(second):
            second[i - lag]()
        if i < len(fill):
            fill[i]()
    twins(0)
    unpack(0)
    signal, spread = levels()
    noise = noise_p[...].astype(f32)
    stream = signal * clean_p[...].astype(f32) + spread * noise
    stream = forward(0, stream)
    twins(1)
    unpack(1)
    stream = forward(1, stream)
    ds = (stream - noise) * (1.0 / math.sqrt(2 * rows_each * ranks))
    ds = backward(1, ds)
    backward(0, ds)

    box[flat] = part[x]

    def give(i):
        return pltpu.make_async_remote_copy(
            src_ref=part.at[i // ranks], dst_ref=box.at[flat], send_sem=all_send.at[0], recv_sem=all_recv.at[0],
            device_id=(i // ranks, i % ranks), device_id_type=MESH,
        )

    @pl.loop(0, devices)
    def _(i):
        @pl.when(i != flat)
        def _():
            give(i).start()

    fetch_p.wait()
    fetch_s.wait()
    rest = box.at[pl.ds(0, devices - 1)]
    pltpu.make_async_copy(rest, rest, all_recv.at[0]).wait()
    grads = jnp.concatenate(
        [jnp.sum(box[0:ranks], axis=0), jnp.sum(box[ranks:devices], axis=0)], axis=0
    )
    where_row = lax.broadcasted_iota(jnp.int32, (8, 1), 0) % 4
    own = jnp.zeros_like(grads)
    for l in range(4):
        own = jnp.where(where_row == l, dot(grads, precond[l], precision=lax.Precision.HIGHEST), own)
    pre[x] = jnp.concatenate([own, jnp.zeros_like(own)], axis=0).astype(bf16)
    swap = pltpu.make_async_remote_copy(
        src_ref=pre.at[x], dst_ref=pre.at[x], send_sem=pre_send.at[0], recv_sem=pre_recv.at[0],
        device_id=(far, me), device_id_type=MESH,
    )
    swap.start()
    swap.wait()
    low = jnp.zeros((1, raw_ref.shape[1]), f32)
    high = jnp.zeros((1, raw_ref.shape[1]), f32)
    for h in range(2):
        for l in range(4):
            at = 4 * h + l
            r = dot_t(pre[h], store[:, 256 * at : 256 * (at + 1)])
            low += r[l : l + 1]
            high += r[4 + l : 5 + l]
    raw_ref[...] = jnp.concatenate([low, high], axis=0)

    pltpu.make_async_copy(rest, rest, all_send.at[0]).wait()
    for guard, what in started:
        def done(what=what):
            copy(*what).wait_send()
        if guard is None:
            done()
        else:
            pl.when(guard)(done)


def fused(
    clean_feats, noise_draw, timesteps, weight_in, weight_ffin, weight_ffout, weight_out, norm_gain, norm_bias,
    sketch_cin, sketch_fin, sketch_cout, sketch_fout, precond, store_grads, store_scale,
):
    channels = clean_feats.shape[-1]
    rows = clean_feats.shape[1] * clean_feats.shape[2]
    hidden = sketch_fin.shape[1]
    width = sketch_cin.shape[-1] ** 2
    vmem = pl.BlockSpec(memory_space=pltpu.VMEM)
    anywhere = pl.BlockSpec(memory_space=pl.ANY)
    raw = pl.pallas_call(
        kernel,
        out_shape=jax.ShapeDtypeStruct((2, store_grads.shape[0]), f32),
        in_specs=[pl.BlockSpec(memory_space=pltpu.SMEM)] + [vmem] * 12 + [anywhere] * 2,
        out_specs=vmem,
        scratch_shapes=[
            pltpu.VMEM((2, ranks, slot, lanes), bf16),
            pltpu.VMEM((2, 2, lanes, lanes), bf16),
            pltpu.VMEM((2, lanes, hidden), bf16),
            pltpu.VMEM((rows, lanes), bf16),
            pltpu.VMEM((rows, lanes), bf16),
            pltpu.VMEM((2, lanes), f32),
            pltpu.VMEM((2, lanes), f32),
            pltpu.VMEM((2, 3, width, lanes), bf16),
            pltpu.VMEM((2, width, hidden), bf16),
            pltpu.VMEM((2, 3, width, lanes), bf16),
            pltpu.VMEM((2, 2, width, hidden), bf16),
            pltpu.VMEM((2, rows, lanes), bf16),
            pltpu.VMEM((2, rows, lanes), f32),
            pltpu.VMEM((2, rows, 1), f32),
            pltpu.VMEM((2, rows, lanes), bf16),
            pltpu.VMEM((2, rows, hidden), f32),
            pltpu.VMEM((2, rows, hidden), f32),
            pltpu.VMEM((2, rows, hidden), bf16),
            pltpu.VMEM((2, rows, lanes), bf16),
            pltpu.VMEM((2, 4, width), f32),
            pltpu.VMEM((2 * ranks, 4, width), f32),
            pltpu.VMEM((2, 16, width), bf16),
            pltpu.VMEM(precond.shape, f32),
            pltpu.VMEM(store_grads.shape, bf16),
            pltpu.SemaphoreType.DMA((4, 2, ranks, 2)),
            pltpu.SemaphoreType.DMA((2, ranks, 2)),
            pltpu.SemaphoreType.DMA((1,)),
            pltpu.SemaphoreType.DMA((1,)),
            pltpu.SemaphoreType.DMA((1,)),
            pltpu.SemaphoreType.DMA((1,)),
            pltpu.SemaphoreType.DMA((2,)),
        ],
        compiler_params=pltpu.CompilerParams(
            collective_id=0, has_side_effects=True, vmem_limit_bytes=60 * 1024 * 1024
        ),
    )(
        timesteps.reshape(-1), clean_feats.reshape(rows, channels), noise_draw.reshape(rows, channels),
        weight_in, weight_ffin, weight_ffout, weight_out, norm_gain, norm_bias,
        sketch_cin, sketch_fin, sketch_cout, sketch_fout, precond, store_grads,
    )
    return raw * store_scale[None, :]


def solution(mesh):
    placed = (
        P("query", None, "corpus", None),
        P("query", None, "corpus", None),
        P("query", None),
        P(None, None, "corpus"),
        P(None, None, "corpus"),
        P(None, None, "corpus"),
        P(None, None, "corpus"),
        P(),
        P(),
        P(),
        P(),
        P(),
        P(),
        P("query", None, None),
        P(("query", "corpus"), None),
        P(("query", "corpus")),
    )
    planned = mesh.shape["query"] == 2 and mesh.shape["corpus"] == ranks
    return jax.shard_map(
        fused if planned else on_device,
        mesh=mesh,
        in_specs=placed,
        out_specs=P(None, ("query", "corpus")),
        check_vma=False,
    )
```
